512 devices in a mesh: child: 8 (over z_lo), prow: 8 (over z_hi, x), pcol: 8 (over y, core).
Axes of the slice: x: 4, y: 4, z: 16 (z_hi: 2, z_lo: 8; z = z_hi * 8 + z_lo), core: 2. Of those that a mesh axis runs over, the one named last changes fastest.
Arguments:
- parent_inverse: float32 [8, 8, 128, 8, 8, 128], P('child', 'prow', None, None, 'pcol'), may hold values from -6 to 6
- child_blocks: int32 [8, 32], replicated, may hold values from -1 to 63, as said below
- factor_rows: float32 [8, 4, 8, 128, 2048], P('child', None, 'prow', None, 'pcol'), may hold values from -0.09375 to 0.09375
- diag_inverse: float32 [8, 2048, 2048], P('child', 'prow', 'pcol'), may hold values from -6 to 6
Outputs:
- inverse_rows: float32 [8, 4, 8, 128, 2048], P('child', None, 'prow', None, 'pcol')
- inverse_diag: float32 [8, 2048, 2048], P('child', 'prow', 'pcol')
The draws below stay inside these ranges and needn't reach their ends.
Inputs may be any that keep to these rules, and one draw needn't show every extreme that they name: `child_blocks`: entry j of a child's list is -1 (padding) or a parent block congruent to j modulo 8; no child names a block twice.
All inputs are finite; a program needn't handle non-finite values.
Results may differ from the reference program's by a relative error of at most 0.0003.
Values sent between devices are 32-bit elements; how exact they have to be, the bound alone decides.
No kernel may reach another device: no remote copies, remote signals or barrier semaphores. Data moves between devices by JAX's collectives and lax.ppermute only.
A program may use at most 64 MiB of HBM per device.

```python
import jax
import jax.numpy as jnp
from jax import lax

BLK = 128
K = 2048
NBI = 32
NBP = 64
CHILDREN = 8
PCOLS = 8
N_PROW = 8
N_PCOL = 8


def draw_child_blocks(key, part):
    key = jax.random.fold_in(key, 11)
    key_scores = jax.random.fold_in(key, 1)
    key_alive = jax.random.fold_in(key, 2)
    per_class = NBP // PCOLS
    class_slots = NBI // PCOLS
    raw_scores = jax.random.randint(key_scores, (CHILDREN, PCOLS, per_class), 0, 1 << 20, dtype=jnp.int32)
    candidate = jnp.arange(per_class, dtype=jnp.int32)[None, None, :]
    child_iota = jnp.arange(CHILDREN, dtype=jnp.int32)[:, None, None]
    column_class = jnp.arange(PCOLS, dtype=jnp.int32)[None, :, None]
    scores = raw_scores * per_class + candidate
    forced = (child_iota == 0) & (column_class == PCOLS - 1) & (candidate == per_class - 1)
    scores = jnp.where(forced, -1, scores)
    ranking = jnp.argsort(scores, axis=-1, stable=True)[:, :, :class_slots].astype(jnp.int32)
    blocks = ranking * PCOLS + column_class
    alive_mask = jax.random.randint(key_alive, (CHILDREN, PCOLS, class_slots), 0, 4, dtype=jnp.int32) > 0
    slot_iota = jnp.arange(class_slots, dtype=jnp.int32)[None, None, :]
    keep_alive = (child_iota == 0) & (column_class == PCOLS - 1) & (slot_iota == 0)
    keep_dead = (child_iota == CHILDREN - 1) & (column_class == 0) & (slot_iota == 0)
    alive_mask = (alive_mask | keep_alive) & jnp.logical_not(keep_dead)
    listed = jnp.where(alive_mask, blocks, -1)
    return jnp.transpose(listed, (0, 2, 1)).reshape(CHILDREN, NBI).astype(jnp.int32)


def level_of(own_key, shape, shards, low, high):
    def one(axis_at, shards_of):
        draws = jax.random.uniform(jax.random.fold_in(jax.random.fold_in(own_key, 6), axis_at), (shards_of,), jnp.float32, low / len(shards), high / len(shards))
        return jnp.repeat(jnp.exp(draws), shape[axis_at] // shards_of).reshape((-1,) + (1,) * (len(shape) - axis_at - 1))

    factor_of = one(*shards[0])
    for cut in shards[1:]:
        factor_of = factor_of * one(*cut)
    return factor_of


def gaussian(stream_key, dims, width, limit, pieces=(), kind=jnp.bfloat16):
    entries = jax.random.normal(stream_key, dims, jnp.float32) * width
    if len(pieces) > 0:
        entries = level_of(stream_key, dims, pieces, -0.22, 0.18) * entries
    return jnp.clip(entries, min=-limit, max=limit).astype(kind)


def setup_inputs(seed: int = 0) -> dict:
    key_list = jax.random.split(jax.random.key(seed), 5)
    parent_inverse = gaussian(key_list[0], (NBP // N_PROW, N_PROW, BLK, NBP // N_PCOL, N_PCOL, BLK), 1.0, 6.0, ((0, 8), (1, 8), (4, 8)), jnp.float32)
    child_blocks = draw_child_blocks(jax.random.fold_in(key_list[4], 71), 0)
    factor_rows = gaussian(key_list[2], (CHILDREN, NBI // N_PROW, N_PROW, BLK, K), (NBI * BLK) ** -0.5, 0.09375, ((0, 8), (2, 8), (4, 8)), jnp.float32)
    diag_inverse = gaussian(key_list[3], (CHILDREN, K, K), 1.0, 6.0, ((0, 8), (1, 8), (2, 8)), jnp.float32)
    return dict(parent_inverse=parent_inverse, child_blocks=child_blocks, factor_rows=factor_rows, diag_inverse=diag_inverse)


def one_child(parent_matrix, block_names, factor, diag_block):
    alive_slots = block_names >= 0
    safe_names = jnp.where(alive_slots, block_names, 0).astype(jnp.int32)
    row_index = (safe_names[:, None] * BLK + jnp.arange(BLK, dtype=jnp.int32)[None, :]).reshape(-1)
    alive_rows = jnp.repeat(alive_slots, BLK)
    restricted = jnp.take(jnp.take(parent_matrix, row_index, axis=0), row_index, axis=1)
    restricted = jnp.where(alive_rows[:, None] & alive_rows[None, :], restricted, jnp.zeros_like(restricted))
    factor = factor.reshape(NBI * BLK, K)
    inverse_rows = -jnp.dot(restricted, factor, precision=lax.Precision.HIGHEST, preferred_element_type=jnp.float32)
    correction = jnp.dot(factor.T, inverse_rows, precision=lax.Precision.HIGHEST, preferred_element_type=jnp.float32)
    return inverse_rows, diag_block - correction


def reference(parent_inverse, child_blocks, factor_rows, diag_inverse):
    parent_matrix = parent_inverse.reshape(NBP * BLK, NBP * BLK)

    def per_child(packed):
        return one_child(parent_matrix, packed[0], packed[1], packed[2])

    rows_out, diag_out = lax.map(per_child, (child_blocks, factor_rows, diag_inverse))
    return rows_out.reshape(CHILDREN, NBI // N_PROW, N_PROW, BLK, K), diag_out
```

```python
import jax
import jax.numpy as jnp
from jax import lax
from jax.experimental import pallas as pl
from jax.experimental.pallas import tpu as pltpu
from jax.sharding import Mesh, PartitionSpec as P

def shift(value, axis, count, step):
    return lax.ppermute(value, axis, [(i, (i - step) % count) for i in range(count)])


def dot(left, right, contract):
    return lax.dot_general(
        left,
        right,
        (contract, ((), ())),
        precision=lax.Precision.HIGH,
        preferred_element_type=jnp.float32,
    )


def pick_kernel(info, row, out):
    slot = pl.program_id(0)
    block = row[0]
    lane = lax.broadcasted_iota(jnp.int32, block.shape, 1)
    for col in range(4):
        place = info[4 + slot * 4 + col]
        out[0, :, col * 128 : (col + 1) * 128] = jnp.sum(
            jnp.where(lane == place, block, 0.0), axis=1
        )


def pick(rows, row_place, places):
    info = jnp.concatenate([row_place, places.reshape(-1)]).astype(jnp.int32)
    return pl.pallas_call(
        pick_kernel,
        out_shape=jax.ShapeDtypeStruct((4, 128, 512), jnp.float32),
        grid_spec=pltpu.PrefetchScalarGridSpec(
            num_scalar_prefetch=1,
            grid=(4,),
            in_specs=[pl.BlockSpec((1, 128, 8, 128), lambda i, info: (info[i], 0, 0, 0))],
            out_specs=pl.BlockSpec((1, 128, 512), lambda i, info: (i, 0, 0)),
        ),
        compiler_params=pltpu.CompilerParams(vmem_limit_bytes=16 << 20),
        cost_estimate=pl.CostEstimate(flops=0, bytes_accessed=3 << 20, transcendentals=0),
        name="pick",
    )(info, rows)


def on_device(parent_inverse, child_blocks, factor_rows, diag_inverse):
    child, half, x, y, core = (
        lax.axis_index(name) for name in ("zl", "zh", "x", "y", "core")
    )
    row_index, col_index = half * 4 + x, y * 2 + core
    own_list = lax.dynamic_index_in_dim(child_blocks, child, 0, keepdims=False).reshape(4, 8)
    row_names = lax.dynamic_index_in_dim(own_list, row_index, 1, keepdims=False)
    col_names = lax.dynamic_index_in_dim(own_list, col_index, 1, keepdims=False)
    row_alive, col_alive = row_names >= 0, col_names >= 0
    row_place = jnp.where(row_alive, row_names, 0) // 8
    col_place = col_names // 8
    places = jnp.where(row_alive[:, None] & col_alive[None], col_place[None], -1)

    factor = factor_rows.reshape(512, 256)
    parent = parent_inverse.reshape(128, 8, 128)
    gathered = lax.all_gather(parent, "zl", axis=0)

    other = shift(factor, "zh", 2, 1)
    lower = jnp.stack([factor] + [shift(factor, "y", 4, j) for j in (1, 2, 3)])
    near = [factor] + [shift(factor, "x", 4, j) for j in (1, 2, 3)]
    lower = jnp.concatenate([lower, shift(lower, "core", 2, 1)])
    far = [other] + [shift(other, "x", 4, j) for j in (1, 2, 3)]

    met = [2 * ((y + j) % 4) + (core + k) % 2 for j in (0, 1, 3, 2) for k in (0, 1)]
    met = jnp.stack(met)
    place = jnp.where(met // 4 == half, 0, 4) + (met % 4 - x) % 4
    panel = jnp.take(jnp.stack(near + far), place, axis=0)

    to_x = jnp.stack([(x + j) % 4 for j in range(4)])
    block = jnp.concatenate([(1 - half) * 4 + to_x, half * 4 + to_x])
    block_place = jnp.where(block % 2 == core, 0, 4) + (block // 2 - y) % 4
    lower = jnp.take(lower, block_place, axis=0)

    restricted = pick(gathered, row_place, places)
    top, bottom = restricted[:2].reshape(256, 512), restricted[2:].reshape(256, 512)
    top_next, bottom_last = shift(top, "y", 4, 1), shift(bottom, "y", 4, 3)
    bottom_next, top_last = shift(bottom, "y", 4, 1), shift(top, "y", 4, 3)
    top_across, bottom_across = shift(top_next, "y", 4, 1), shift(bottom_last, "y", 4, 3)

    def product(pieces):
        total = None
        for i, piece in enumerate(pieces):
            for k, one in enumerate((piece, shift(piece, "core", 2, 1))):
                term = dot(one, panel[2 * i + k], ((1,), (0,)))
                total = term if total is None else total + term
        return -total

    inverse_local = jnp.concatenate(
        [
            product([top, top_next, top_last, top_across]),
            product([bottom, bottom_next, bottom_last, bottom_across]),
        ]
    )

    def spread(first):
        share = [dot(lower[first + j], inverse_local, ((0,), (0,))) for j in range(4)]
        return share[0] + sum(shift(share[j], "x", 4, -j) for j in (1, 2, 3))

    other_half = shift(spread(0), "zh", 2, 1)
    reduced = spread(4) + other_half
    inverse_diag = diag_inverse - reduced[None]
    return inverse_local.reshape(1, 4, 1, 128, 256), inverse_diag


def solution(mesh):
    fine = Mesh(mesh.devices.reshape(8, 2, 4, 4, 2), ("zl", "zh", "x", "y", "core"))
    rows, cols = ("zh", "x"), ("y", "core")
    in_specs = (
        P("zl", rows, None, None, cols, None),
        P(),
        P("zl", None, rows, None, cols),
        P("zl", rows, cols),
    )
    out_specs = (P("zl", None, rows, None, cols), P("zl", rows, cols))
    return jax.shard_map(
        on_device, mesh=fine, in_specs=in_specs, out_specs=out_specs, check_vma=False
    )
```

```python
import functools

import jax
import jax.numpy as jnp
from jax import lax
from jax.experimental import pallas as pl
from jax.experimental.pallas import tpu as pltpu
from jax.sharding import Mesh, PartitionSpec as P

def shift(value, axis, count, step):
    return lax.ppermute(value, axis, [(i, (i - step) % count) for i in range(count)])


def dot(left, right, contract):
    return lax.dot_general(
        left,
        right,
        (contract, ((), ())),
        precision=lax.Precision.HIGH,
        preferred_element_type=jnp.float32,
    )


def pick_kernel(info, row, out):
    slot = pl.program_id(0)
    for col in range(4):
        place = info[4 + slot * 4 + col]
        found = row[0, pl.ds(jnp.maximum(place, 0), 128, stride=8), :]
        out[col // 2, :, col % 2 * 128 : (col % 2 + 1) * 128] = jnp.where(
            place >= 0, found, 0.0
        )


def pick(rows, row_place, places):
    info = jnp.concatenate([row_place, places.reshape(-1)]).astype(jnp.int32)
    return pl.pallas_call(
        pick_kernel,
        out_shape=jax.ShapeDtypeStruct((2, 512, 256), jnp.float32),
        grid_spec=pltpu.PrefetchScalarGridSpec(
            num_scalar_prefetch=1,
            grid=(4,),
            in_specs=[pl.BlockSpec((1, 1024, 128), lambda i, info: (info[i], 0, 0))],
            out_specs=pl.BlockSpec((2, 128, 256), lambda i, info: (0, i, 0)),
        ),
        compiler_params=pltpu.CompilerParams(vmem_limit_bytes=56 << 20),
        cost_estimate=pl.CostEstimate(flops=0, bytes_accessed=3 << 20, transcendentals=0),
        name="pick",
    )(info, rows.reshape(8, 1024, 128))


def two_halves(value):
    high = value.astype(jnp.bfloat16)
    return high, (value - high.astype(jnp.float32)).astype(jnp.bfloat16)


def product_kernel(terms, count, has_base, classes, *refs):
    restricted, panels = refs[0], refs[1 : 1 + count]
    out, left, right, left_sems, right_sems = refs[1 + count + has_base :]

    def copies(n):
        index, panel, start, k = terms[n]
        yield pltpu.make_async_copy(
            restricted.at[classes[index], k], left.at[n], left_sems.at[n]
        )
        yield pltpu.make_async_copy(
            panels[panel].at[pl.ds(start, 256)], right.at[n], right_sems.at[n]
        )

    for n in range(len(terms)):
        for copy in copies(n):
            copy.start()
    for n in range(len(terms)):
        for copy in copies(n):
            copy.wait()
        if n > 0:
            total = out[...]
        elif has_base:
            total = refs[1 + count][...]
        else:
            total = jnp.zeros(out.shape, jnp.float32)
        lh, ll = two_halves(left[n])
        rh, rl = two_halves(right[n])
        for one, two in ((lh, rh), (lh, rl), (ll, rh)):
            total -= jnp.dot(one, two, preferred_element_type=jnp.float32)
        out[...] = total


def product(restricted, panels, classes, terms, base=None):
    has_base = base is not None
    whole = pl.BlockSpec(memory_space=pltpu.VMEM)
    return pl.pallas_call(
        functools.partial(product_kernel, terms, len(panels), has_base),
        out_shape=jax.ShapeDtypeStruct((512, 256), jnp.float32),
        grid_spec=pltpu.PrefetchScalarGridSpec(
            num_scalar_prefetch=1,
            grid=(),
            in_specs=[pl.BlockSpec(memory_space=pl.ANY)] * (1 + len(panels))
            + [whole] * has_base,
            out_specs=whole,
            scratch_shapes=[
                pltpu.VMEM((len(terms), 512, 256), jnp.float32),
                pltpu.VMEM((len(terms), 256, 256), jnp.float32),
                pltpu.SemaphoreType.DMA((len(terms),)),
                pltpu.SemaphoreType.DMA((len(terms),)),
            ],
        ),
        compiler_params=pltpu.CompilerParams(vmem_limit_bytes=28 << 20),
        cost_estimate=pl.CostEstimate(
            flops=len(terms) * (3 << 26),
            bytes_accessed=len(terms) * (3 << 18),
            transcendentals=0,
        ),
        name="product",
    )(classes, restricted, *panels, *([base] if has_base else []))


def on_device(parent_inverse, child_blocks, factor_rows, diag_inverse):
    child, half, x, y, core = (
        lax.axis_index(name) for name in ("zl", "zh", "x", "y", "core")
    )
    row_index, col_index = half * 4 + x, y * 2 + core
    own_list = lax.dynamic_index_in_dim(child_blocks, child, 0, keepdims=False).reshape(4, 8)
    row_names = lax.dynamic_index_in_dim(own_list, row_index, 1, keepdims=False)
    col_names = lax.dynamic_index_in_dim(own_list, col_index, 1, keepdims=False)
    row_alive, col_alive = row_names >= 0, col_names >= 0
    row_place = jnp.where(row_alive, row_names, 0) // 8
    col_place = col_names // 8
    places = jnp.where(row_alive[:, None] & col_alive[None], col_place[None], -1)

    factor = factor_rows.reshape(512, 256)
    parent = parent_inverse.reshape(128, 8, 128)
    gathered = lax.all_gather(parent, "zl", axis=0)

    lower = jnp.stack([factor] + [shift(factor, "y", 4, j) for j in (1, 2, 3)])
    near = [factor] + [shift(factor, "x", 4, j) for j in (1, 2, 3)]
    lower = jnp.concatenate([lower, shift(lower, "core", 2, 1)])
    to_x = jnp.stack([(x + j) % 4 for j in range(4)])
    block = jnp.concatenate([(1 - half) * 4 + to_x, half * 4 + jnp.arange(4)])
    block_place = jnp.where(block % 2 == core, 0, 4) + (block // 2 - y) % 4
    lower = jnp.take(lower, block_place, axis=0, mode="clip")
    gathered, top, bottom, lower, near = lax.optimization_barrier(
        (gathered, factor[:256], factor[256:], lower, near)
    )

    restricted = pick(gathered, row_place, places)
    restricted = lax.all_gather(restricted, ("y", "core"), axis=0)
    top, bottom = lax.optimization_barrier((shift(top, "zh", 2, 1), bottom))
    bottom = shift(bottom, "zh", 2, 1)
    far_top = [top] + [shift(top, "x", 4, j) for j in (1, 2, 3)]
    far_bottom = [bottom] + [shift(bottom, "x", 4, j) for j in (1, 2, 3)]

    classes = jnp.concatenate([half * 4 + to_x, (1 - half) * 4 + to_x]).astype(jnp.int32)
    terms = [(j, j, 256 * k, k) for j in range(4) for k in (0, 1)]
    terms += [(4 + j, 4 + j, 0, 0) for j in range(4)]
    inverse_local = product(restricted, near + far_top, classes, terms)
    terms = [(4 + j, j, 0, 1) for j in range(4)]
    inverse_local = product(restricted, far_bottom, classes, terms, inverse_local)

    share = [dot(lower[j], inverse_local, ((0,), (0,))) for j in range(4)]
    *share, own_lower = lax.optimization_barrier((*share, lower[4:]))
    other_half = share[0] + sum(shift(share[j], "x", 4, -j) for j in (1, 2, 3))
    other_half = shift(other_half, "zh", 2, 1)
    share = [dot(own_lower[j], inverse_local, ((0,), (0,))) for j in range(4)]
    own_half = lax.psum_scatter(jnp.stack(share), "x", scatter_dimension=0)
    reduced = own_half + other_half
    inverse_diag = diag_inverse - reduced[None]
    return inverse_local.reshape(1, 4, 1, 128, 256), inverse_diag


def solution(mesh):
    fine = Mesh(mesh.devices.reshape(8, 2, 4, 4, 2), ("zl", "zh", "x", "y", "core"))
    rows, cols = ("zh", "x"), ("y", "core")
    in_specs = (
        P("zl", rows, None, None, cols, None),
        P(),
        P("zl", None, rows, None, cols),
        P("zl", rows, cols),
    )
    out_specs = (P("zl", None, rows, None, cols), P("zl", rows, cols))
    return jax.shard_map(
        on_device, mesh=fine, in_specs=in_specs, out_specs=out_specs, check_vma=False
    )
```

```python
import functools

import jax
import jax.numpy as jnp
from jax import lax
from jax.experimental import pallas as pl
from jax.experimental.pallas import tpu as pltpu
from jax.sharding import Mesh, PartitionSpec as P

def shift(value, axis, count, step):
    return lax.ppermute(value, axis, [(i, (i - step) % count) for i in range(count)])


def dot(left, right, contract):
    return lax.dot_general(
        left,
        right,
        (contract, ((), ())),
        precision=lax.Precision.HIGH,
        preferred_element_type=jnp.float32,
    )


def column_block(row, place):
    found = row[pl.ds(jnp.maximum(place, 0), 128, stride=8), :]
    return jnp.where(place >= 0, found, 0.0)


def trim_kernel(info, up, down, *refs):
    outs, held, sem = refs[:3], refs[3], refs[4]
    for n, row in enumerate((up, down)):

        @pl.when(info[0] == n)
        def _():
            pltpu.make_async_copy(row, held, sem).start()

    pltpu.make_async_copy(up, held, sem).wait()
    for n, out in enumerate(outs):
        for col in range(4):
            out[:, col * 128 : (col + 1) * 128] = column_block(held, info[1 + n * 4 + col])


def trim(up, down, side, places):
    info = jnp.concatenate([side[None], places.reshape(-1)]).astype(jnp.int32)
    return pl.pallas_call(
        trim_kernel,
        out_shape=[jax.ShapeDtypeStruct((128, 512), jnp.float32)] * 3,
        grid_spec=pltpu.PrefetchScalarGridSpec(
            num_scalar_prefetch=1,
            grid=(),
            in_specs=[pl.BlockSpec(memory_space=pl.ANY)] * 2,
            out_specs=[pl.BlockSpec(memory_space=pltpu.VMEM)] * 3,
            scratch_shapes=[
                pltpu.VMEM((1024, 128), jnp.float32),
                pltpu.SemaphoreType.DMA,
            ],
        ),
        compiler_params=pltpu.CompilerParams(vmem_limit_bytes=16 << 20),
        cost_estimate=pl.CostEstimate(flops=0, bytes_accessed=5 << 18, transcendentals=0),
        name="trim",
    )(info, up, down)


def pick_kernel(info, *refs):
    rows, cut, out, held, held_cut, sems = refs[:9], refs[9:12], *refs[12:]
    for slot in range(4):
        for n in range(12):

            @pl.when(info[slot] == n)
            def _():
                if n < 9:
                    pltpu.make_async_copy(rows[n], held.at[slot], sems.at[slot]).start()
                else:
                    pltpu.make_async_copy(
                        cut[n - 9], held_cut.at[slot], sems.at[slot]
                    ).start()

    for slot in range(4):
        here = slice(slot * 128, (slot + 1) * 128)

        @pl.when(info[slot] < 9)
        def _():
            pltpu.make_async_copy(rows[0], held.at[slot], sems.at[slot]).wait()
            for col in range(4):
                out[col // 2, here, col % 2 * 128 : (col % 2 + 1) * 128] = column_block(
                    held.at[slot], info[4 + slot * 4 + col]
                )

        @pl.when(info[slot] >= 9)
        def _():
            pltpu.make_async_copy(cut[0], held_cut.at[slot], sems.at[slot]).wait()
            for k in range(2):
                out[k, here, :] = held_cut[slot, :, k * 256 : (k + 1) * 256]


def pick(rows, cut, source, places):
    info = jnp.concatenate([source, places.reshape(-1)]).astype(jnp.int32)
    return pl.pallas_call(
        pick_kernel,
        out_shape=jax.ShapeDtypeStruct((2, 512, 256), jnp.float32),
        grid_spec=pltpu.PrefetchScalarGridSpec(
            num_scalar_prefetch=1,
            grid=(),
            in_specs=[pl.BlockSpec(memory_space=pl.ANY)] * 12,
            out_specs=pl.BlockSpec(memory_space=pltpu.VMEM),
            scratch_shapes=[
                pltpu.VMEM((4, 1024, 128), jnp.float32),
                pltpu.VMEM((4, 128, 512), jnp.float32),
                pltpu.SemaphoreType.DMA((4,)),
            ],
        ),
        compiler_params=pltpu.CompilerParams(vmem_limit_bytes=56 << 20),
        cost_estimate=pl.CostEstimate(flops=0, bytes_accessed=3 << 20, transcendentals=0),
        name="pick",
    )(info, *rows, *cut)


def two_halves(value):
    high = value.astype(jnp.bfloat16)
    return high, (value - high.astype(jnp.float32)).astype(jnp.bfloat16)


def product_kernel(terms, count, has_base, classes, *refs):
    restricted, panels = refs[0], refs[1 : 1 + count]
    out, left, right, left_sems, right_sems = refs[1 + count + has_base :]

    def copies(n):
        index, panel, start, k = terms[n]
        yield pltpu.make_async_copy(
            restricted.at[classes[index], k], left.at[n], left_sems.at[n]
        )
        yield pltpu.make_async_copy(
            panels[panel].at[pl.ds(start, 256)], right.at[n], right_sems.at[n]
        )

    for n in range(len(terms)):
        for copy in copies(n):
            copy.start()
    for n in range(len(terms)):
        for copy in copies(n):
            copy.wait()
        if n > 0:
            total = out[...]
        elif has_base:
            total = refs[1 + count][...]
        else:
            total = jnp.zeros(out.shape, jnp.float32)
        lh, ll = two_halves(left[n])
        rh, rl = two_halves(right[n])
        for one, two in ((lh, rh), (lh, rl), (ll, rh)):
            total -= jnp.dot(one, two, preferred_element_type=jnp.float32)
        out[...] = total


def product(restricted, panels, classes, terms, base=None):
    has_base = base is not None
    whole = pl.BlockSpec(memory_space=pltpu.VMEM)
    return pl.pallas_call(
        functools.partial(product_kernel, terms, len(panels), has_base),
        out_shape=jax.ShapeDtypeStruct((512, 256), jnp.float32),
        grid_spec=pltpu.PrefetchScalarGridSpec(
            num_scalar_prefetch=1,
            grid=(),
            in_specs=[pl.BlockSpec(memory_space=pl.ANY)] * (1 + len(panels))
            + [whole] * has_base,
            out_specs=whole,
            scratch_shapes=[
                pltpu.VMEM((len(terms), 512, 256), jnp.float32),
                pltpu.VMEM((len(terms), 256, 256), jnp.float32),
                pltpu.SemaphoreType.DMA((len(terms),)),
                pltpu.SemaphoreType.DMA((len(terms),)),
            ],
        ),
        compiler_params=pltpu.CompilerParams(vmem_limit_bytes=28 << 20),
        cost_estimate=pl.CostEstimate(
            flops=len(terms) * (3 << 26),
            bytes_accessed=len(terms) * (3 << 18),
            transcendentals=0,
        ),
        name="product",
    )(classes, restricted, *panels, *([base] if has_base else []))


def on_device(parent_inverse, child_blocks, factor_rows, diag_inverse):
    child, half, x, y, core = (
        lax.axis_index(name) for name in ("zl", "zh", "x", "y", "core")
    )
    row_index, col_index = half * 4 + x, y * 2 + core
    lists = child_blocks.reshape(8, 4, 8)
    own_list = lax.dynamic_index_in_dim(lists, child, 0, keepdims=False)
    row_names = lax.dynamic_index_in_dim(own_list, row_index, 1, keepdims=False)
    col_names = lax.dynamic_index_in_dim(lists, col_index, 2, keepdims=False)
    row_alive = row_names >= 0
    col_place = jnp.where(col_names >= 0, col_names // 8, -1)
    offset = jnp.where(row_alive, row_names // 8 - child, 0)
    away = jnp.abs(offset)
    source = jnp.where(
        away > 4, away + 4, jnp.where(offset < 0, 2 * away - 1, 2 * away)
    )
    places = jnp.where(
        row_alive[:, None],
        lax.dynamic_index_in_dim(col_place, child, 0, keepdims=True),
        -1,
    )

    factor = factor_rows.reshape(512, 256)
    lower = lax.all_gather(factor, ("y", "core"), axis=0)
    near = lax.all_gather(factor, "x", axis=0).reshape(2048, 256)

    up = down = parent_inverse.reshape(1024, 128)
    rows = [up]
    for _ in range(4):
        up = lax.ppermute(up, "zl", [(i, i + 1) for i in range(7)])
        down = lax.ppermute(down, "zl", [(i + 1, i) for i in range(7)])
        up, down = lax.optimization_barrier((up, down))
        rows += [up, down]
    side = (child < 4).astype(jnp.int32)
    further = child + (1 - 2 * side) * jnp.arange(1, 4, dtype=jnp.int32)
    asked = jnp.take(col_place, jnp.clip(further, 0, 7), axis=0, mode="clip")
    cut = [
        lax.ppermute(
            part,
            "zl",
            [(i, i + d) for i in range(4, 8 - d)] + [(i, i - d) for i in range(d, 4)],
        )
        for d, part in zip((1, 2, 3), trim(up, down, side, asked))
    ]

    to_x = jnp.stack([(x + j) % 4 for j in range(4)])
    block = jnp.concatenate([(1 - half) * 4 + to_x, half * 4 + to_x])
    *cut, top, bottom, lower, near = lax.optimization_barrier(
        (*cut, factor[:256], factor[256:], lower, near)
    )

    restricted = pick(rows, cut, source, places)
    restricted, lower = lax.optimization_barrier((restricted, lower))
    lower = jnp.take(lower, block, axis=0, mode="clip")
    lower, top = lax.optimization_barrier((lower, top))
    restricted = lax.all_gather(restricted, ("y", "core"), axis=0)
    top, bottom = lax.optimization_barrier((shift(top, "zh", 2, 1), bottom))
    bottom = shift(bottom, "zh", 2, 1)
    far_top = [top] + [shift(top, "x", 4, j) for j in (1, 2, 3)]

    number = jnp.arange(4, dtype=jnp.int32)
    classes = jnp.concatenate([half * 4 + number, (1 - half) * 4 + to_x]).astype(jnp.int32)
    terms = [(j, 0, 512 * j + 256 * k, k) for j in range(4) for k in (0, 1)]
    terms += [(4 + j, 1 + j, 0, 0) for j in range(4)]
    inverse_local = product(restricted, [near] + far_top, classes, terms)
    far_bottom = [bottom] + [shift(bottom, "x", 4, j) for j in (1, 2, 3)]
    terms = [(4 + j, j, 0, 1) for j in range(4)]
    inverse_local = product(restricted, far_bottom, classes, terms, inverse_local)

    share = [dot(lower[j], inverse_local, ((0,), (0,))) for j in range(4)]
    *share, own_lower = lax.optimization_barrier((*share, lower[4:]))
    other_half = share[0] + sum(shift(share[j], "x", 4, -j) for j in (1, 2, 3))
    share = [dot(own_lower[j], inverse_local, ((0,), (0,))) for j in range(4)]
    other_half, *share = lax.optimization_barrier((other_half, *share))
    other_half = shift(other_half, "zh", 2, 1)
    own_half = share[0] + sum(shift(share[j], "x", 4, -j) for j in (1, 2, 3))
    rest, own_half = lax.optimization_barrier((diag_inverse[0] - other_half, own_half))
    inverse_diag = (rest - own_half)[None]
    return inverse_local.reshape(1, 4, 1, 128, 256), inverse_diag


def solution(mesh):
    fine = Mesh(mesh.devices.reshape(8, 2, 4, 4, 2), ("zl", "zh", "x", "y", "core"))
    rows, cols = ("zh", "x"), ("y", "core")
    in_specs = (
        P("zl", rows, None, None, cols, None),
        P(),
        P("zl", None, rows, None, cols),
        P("zl", rows, cols),
    )
    out_specs = (P("zl", None, rows, None, cols), P("zl", rows, cols))
    return jax.shard_map(
        on_device, mesh=fine, in_specs=in_specs, out_specs=out_specs, check_vma=False
    )
```

```python
import functools

import jax
import jax.numpy as jnp
from jax import lax
from jax.experimental import pallas as pl
from jax.experimental.pallas import tpu as pltpu
from jax.sharding import Mesh, PartitionSpec as P

def shift(value, axis, count, step):
    return lax.ppermute(value, axis, [(i, (i - step) % count) for i in range(count)])


def dot(left, right, contract):
    return lax.dot_general(
        left,
        right,
        (contract, ((), ())),
        precision=lax.Precision.HIGH,
        preferred_element_type=jnp.float32,
    )


def column_block(row, place):
    found = row[pl.ds(jnp.maximum(place, 0), 128, stride=8), :]
    return jnp.where(place >= 0, found, 0.0)


def trim_kernel(info, up, down, *refs):
    outs, held, sem = refs[:3], refs[3], refs[4]
    for n, row in enumerate((up, down)):

        @pl.when(info[0] == n)
        def _():
            pltpu.make_async_copy(row, held, sem).start()

    pltpu.make_async_copy(up, held, sem).wait()
    for n, out in enumerate(outs):
        for col in range(4):
            out[:, col * 128 : (col + 1) * 128] = column_block(held, info[1 + n * 4 + col])


def trim(up, down, side, places):
    info = jnp.concatenate([side[None], places.reshape(-1)]).astype(jnp.int32)
    return pl.pallas_call(
        trim_kernel,
        out_shape=[jax.ShapeDtypeStruct((128, 512), jnp.float32)] * 3,
        grid_spec=pltpu.PrefetchScalarGridSpec(
            num_scalar_prefetch=1,
            grid=(),
            in_specs=[pl.BlockSpec(memory_space=pl.ANY)] * 2,
            out_specs=[pl.BlockSpec(memory_space=pltpu.VMEM)] * 3,
            scratch_shapes=[
                pltpu.VMEM((1024, 128), jnp.float32),
                pltpu.SemaphoreType.DMA,
            ],
        ),
        compiler_params=pltpu.CompilerParams(vmem_limit_bytes=16 << 20),
        cost_estimate=pl.CostEstimate(flops=0, bytes_accessed=5 << 18, transcendentals=0),
        name="trim",
    )(info, up, down)


def pick_kernel(info, *refs):
    rows, cut, out, held, held_cut, sems = refs[:9], refs[9:12], *refs[12:]
    for slot in range(4):
        for n in range(12):

            @pl.when(info[slot] == n)
            def _():
                if n < 9:
                    pltpu.make_async_copy(rows[n], held.at[slot], sems.at[slot]).start()
                else:
                    pltpu.make_async_copy(
                        cut[n - 9], held_cut.at[slot], sems.at[slot]
                    ).start()

    for slot in range(4):
        here = slice(slot * 128, (slot + 1) * 128)

        @pl.when(info[slot] < 9)
        def _():
            pltpu.make_async_copy(rows[0], held.at[slot], sems.at[slot]).wait()
            for col in range(4):
                out[col // 2, here, col % 2 * 128 : (col % 2 + 1) * 128] = column_block(
                    held.at[slot], info[4 + slot * 4 + col]
                )

        @pl.when(info[slot] >= 9)
        def _():
            pltpu.make_async_copy(cut[0], held_cut.at[slot], sems.at[slot]).wait()
            for k in range(2):
                out[k, here, :] = held_cut[slot, :, k * 256 : (k + 1) * 256]


def pick(rows, cut, source, places):
    info = jnp.concatenate([source, places.reshape(-1)]).astype(jnp.int32)
    return pl.pallas_call(
        pick_kernel,
        out_shape=jax.ShapeDtypeStruct((2, 512, 256), jnp.float32),
        grid_spec=pltpu.PrefetchScalarGridSpec(
            num_scalar_prefetch=1,
            grid=(),
            in_specs=[pl.BlockSpec(memory_space=pl.ANY)] * 12,
            out_specs=pl.BlockSpec(memory_space=pltpu.VMEM),
            scratch_shapes=[
                pltpu.VMEM((4, 1024, 128), jnp.float32),
                pltpu.VMEM((4, 128, 512), jnp.float32),
                pltpu.SemaphoreType.DMA((4,)),
            ],
        ),
        compiler_params=pltpu.CompilerParams(vmem_limit_bytes=56 << 20),
        cost_estimate=pl.CostEstimate(flops=0, bytes_accessed=3 << 20, transcendentals=0),
        name="pick",
    )(info, *rows, *cut)


def two_halves(value):
    high = value.astype(jnp.bfloat16)
    return high, (value - high.astype(jnp.float32)).astype(jnp.bfloat16)


def product_kernel(terms, count, last, classes, *refs):
    restricted, panels = refs[0], refs[1 : 1 + count]
    if last:
        base, lower, out, share, left, right, left_sems, right_sems, held, sem = refs[
            1 + count :
        ]
    else:
        out, left, right, left_sems, right_sems = refs[1 + count :]

    def copies(n):
        index, panel, start, k = terms[n]
        yield pltpu.make_async_copy(
            restricted.at[classes[index], k], left.at[n], left_sems.at[n]
        )
        yield pltpu.make_async_copy(
            panels[panel].at[pl.ds(start, 256)], right.at[n], right_sems.at[n]
        )

    for n in range(len(terms)):
        for copy in copies(n):
            copy.start()
    if last:
        held_copy = pltpu.make_async_copy(lower, held, sem)
        held_copy.start()
    for n in range(len(terms)):
        for copy in copies(n):
            copy.wait()
        if n > 0:
            total = out[...]
        elif last:
            total = base[...]
        else:
            total = jnp.zeros(out.shape, jnp.float32)
        lh, ll = two_halves(left[n])
        rh, rl = two_halves(right[n])
        for one, two in ((lh, rh), (lh, rl), (ll, rh)):
            total -= jnp.dot(one, two, preferred_element_type=jnp.float32)
        out[...] = total
    if last:
        held_copy.wait()
        rh, rl = two_halves(out[...])
        for j in range(4):
            lh, ll = two_halves(held[j])
            total = jnp.zeros((256, 256), jnp.float32)
            for one, two in ((lh, rh), (lh, rl), (ll, rh)):
                total += jnp.dot(one, two, preferred_element_type=jnp.float32)
            share[j] = total


def product(restricted, panels, classes, terms, base=None, lower=None):
    last = base is not None
    whole, there = pl.BlockSpec(memory_space=pltpu.VMEM), pl.BlockSpec(memory_space=pl.ANY)
    out_shape = [jax.ShapeDtypeStruct((512, 256), jnp.float32)]
    scratch = [
        pltpu.VMEM((len(terms), 512, 256), jnp.float32),
        pltpu.VMEM((len(terms), 256, 256), jnp.float32),
        pltpu.SemaphoreType.DMA((len(terms),)),
        pltpu.SemaphoreType.DMA((len(terms),)),
    ]
    if last:
        out_shape += [jax.ShapeDtypeStruct((4, 256, 256), jnp.float32)]
        scratch += [pltpu.VMEM((4, 256, 512), jnp.float32), pltpu.SemaphoreType.DMA]
    return pl.pallas_call(
        functools.partial(product_kernel, terms, len(panels), last),
        out_shape=out_shape,
        grid_spec=pltpu.PrefetchScalarGridSpec(
            num_scalar_prefetch=1,
            grid=(),
            in_specs=[there] * (1 + len(panels)) + [whole, there] * last,
            out_specs=[whole] * len(out_shape),
            scratch_shapes=scratch,
        ),
        compiler_params=pltpu.CompilerParams(vmem_limit_bytes=56 << 20),
        cost_estimate=pl.CostEstimate(
            flops=len(terms) * (3 << 26),
            bytes_accessed=len(terms) * (3 << 18),
            transcendentals=0,
        ),
        name="product",
    )(classes, restricted, *panels, *([base, lower] if last else []))


def on_device(parent_inverse, child_blocks, factor_rows, diag_inverse):
    child, half, x, y, core = (
        lax.axis_index(name) for name in ("zl", "zh", "x", "y", "core")
    )
    row_index, col_index = half * 4 + x, y * 2 + core
    lists = child_blocks.reshape(8, 4, 8)
    own_list = lax.dynamic_index_in_dim(lists, child, 0, keepdims=False)
    row_names = lax.dynamic_index_in_dim(own_list, row_index, 1, keepdims=False)
    col_names = lax.dynamic_index_in_dim(lists, col_index, 2, keepdims=False)
    row_alive = row_names >= 0
    col_place = jnp.where(col_names >= 0, col_names // 8, -1)
    offset = jnp.where(row_alive, row_names // 8 - child, 0)
    away = jnp.abs(offset)
    source = jnp.where(
        away > 4, away + 4, jnp.where(offset < 0, 2 * away - 1, 2 * away)
    )
    places = jnp.where(
        row_alive[:, None],
        lax.dynamic_index_in_dim(col_place, child, 0, keepdims=True),
        -1,
    )

    factor = factor_rows.reshape(512, 256)
    lower = lax.all_gather(factor, ("y", "core"), axis=0)
    near = lax.all_gather(factor, "x", axis=0).reshape(2048, 256)

    up = down = parent_inverse.reshape(1024, 128)
    rows = [up]
    for _ in range(4):
        up = lax.ppermute(up, "zl", [(i, i + 1) for i in range(7)])
        down = lax.ppermute(down, "zl", [(i + 1, i) for i in range(7)])
        up, down = lax.optimization_barrier((up, down))
        rows += [up, down]
    side = (child < 4).astype(jnp.int32)
    further = child + (1 - 2 * side) * jnp.arange(1, 4, dtype=jnp.int32)
    asked = jnp.take(col_place, jnp.clip(further, 0, 7), axis=0, mode="clip")
    cut = [
        lax.ppermute(
            part,
            "zl",
            [(i, i + d) for i in range(4, 8 - d)] + [(i, i - d) for i in range(d, 4)],
        )
        for d, part in zip((1, 2, 3), trim(up, down, side, asked))
    ]

    to_x = jnp.stack([(x + j) % 4 for j in range(4)])
    *cut, top, bottom, lower, near = lax.optimization_barrier(
        (*cut, factor[:256], factor[256:], lower, near)
    )

    restricted = pick(rows, cut, source, places)
    restricted, lower = lax.optimization_barrier((restricted, lower))
    far_lower = jnp.take(lower, (1 - half) * 4 + to_x, axis=0, mode="clip")
    own_lower = jnp.take(lower, half * 4 + to_x, axis=0, mode="clip")
    far_lower, top = lax.optimization_barrier((far_lower.transpose(0, 2, 1), top))
    restricted = lax.all_gather(restricted, ("y", "core"), axis=0)
    top, bottom = lax.optimization_barrier((shift(top, "zh", 2, 1), bottom))
    bottom = shift(bottom, "zh", 2, 1)
    far_top = [top] + [shift(top, "x", 4, j) for j in (1, 2, 3)]

    number = jnp.arange(4, dtype=jnp.int32)
    classes = jnp.concatenate([half * 4 + number, (1 - half) * 4 + to_x]).astype(jnp.int32)
    terms = [(j, 0, 512 * j + 256 * k, k) for j in range(4) for k in (0, 1)]
    terms += [(4 + j, 1 + j, 0, 0) for j in range(4)]
    (inverse_local,) = product(restricted, [near] + far_top, classes, terms)
    far_bottom = [bottom] + [shift(bottom, "x", 4, j) for j in (1, 2, 3)]
    terms = [(4 + j, j, 0, 1) for j in range(4)]
    inverse_local, share = product(
        restricted, far_bottom, classes, terms, inverse_local, far_lower
    )

    others = [shift(share[j], "x", 4, -j) for j in (1, 2, 3)]
    others[0], own_lower = lax.optimization_barrier((others[0], own_lower))
    other_half = share[0] + sum(others)
    share = [dot(own_lower[j], inverse_local, ((0,), (0,))) for j in range(4)]
    other_half, *share = lax.optimization_barrier((other_half, *share))
    other_half = shift(other_half, "zh", 2, 1)
    own_half = share[0] + sum(shift(share[j], "x", 4, -j) for j in (1, 2, 3))
    rest, own_half = lax.optimization_barrier((diag_inverse[0] - other_half, own_half))
    inverse_diag = (rest - own_half)[None]
    return inverse_local.reshape(1, 4, 1, 128, 256), inverse_diag


def solution(mesh):
    fine = Mesh(mesh.devices.reshape(8, 2, 4, 4, 2), ("zl", "zh", "x", "y", "core"))
    rows, cols = ("zh", "x"), ("y", "core")
    in_specs = (
        P("zl", rows, None, None, cols, None),
        P(),
        P("zl", None, rows, None, cols),
        P("zl", rows, cols),
    )
    out_specs = (P("zl", None, rows, None, cols), P("zl", rows, cols))
    return jax.shard_map(
        on_device, mesh=fine, in_specs=in_specs, out_specs=out_specs, check_vma=False
    )
```

```python
import functools

import jax
import jax.numpy as jnp
from jax import lax
from jax.experimental import pallas as pl
from jax.experimental.pallas import tpu as pltpu
from jax.sharding import Mesh, PartitionSpec as P

def shift(value, axis, count, step):
    return lax.ppermute(value, axis, [(i, (i - step) % count) for i in range(count)])


def dot(left, right, contract):
    return lax.dot_general(
        left,
        right,
        (contract, ((), ())),
        precision=lax.Precision.HIGH,
        preferred_element_type=jnp.float32,
    )


def column_block(row, place):
    found = row[pl.ds(jnp.maximum(place, 0), 128, stride=8), :]
    return jnp.where(place >= 0, found, 0.0)


def trim_kernel(info, up, down, *refs):
    outs, held, sem = refs[:3], refs[3], refs[4]
    for n, row in enumerate((up, down)):

        @pl.when(info[0] == n)
        def _():
            pltpu.make_async_copy(row, held, sem).start()

    pltpu.make_async_copy(up, held, sem).wait()
    for n, out in enumerate(outs):
        for col in range(4):
            out[:, col * 128 : (col + 1) * 128] = column_block(held, info[1 + n * 4 + col])


def trim(up, down, side, places):
    info = jnp.concatenate([side[None], places.reshape(-1)]).astype(jnp.int32)
    return pl.pallas_call(
        trim_kernel,
        out_shape=[jax.ShapeDtypeStruct((128, 512), jnp.float32)] * 3,
        grid_spec=pltpu.PrefetchScalarGridSpec(
            num_scalar_prefetch=1,
            grid=(),
            in_specs=[pl.BlockSpec(memory_space=pl.ANY)] * 2,
            out_specs=[pl.BlockSpec(memory_space=pltpu.VMEM)] * 3,
            scratch_shapes=[
                pltpu.VMEM((1024, 128), jnp.float32),
                pltpu.SemaphoreType.DMA,
            ],
        ),
        compiler_params=pltpu.CompilerParams(vmem_limit_bytes=16 << 20),
        cost_estimate=pl.CostEstimate(flops=0, bytes_accessed=5 << 18, transcendentals=0),
        name="trim",
    )(info, up, down)


def pick_kernel(info, *refs):
    rows, cut, out, held, held_cut, sems = refs[:9], refs[9:12], *refs[12:]
    for slot in range(4):
        for n in range(12):

            @pl.when(info[slot] == n)
            def _():
                if n < 9:
                    pltpu.make_async_copy(rows[n], held.at[slot], sems.at[slot]).start()
                else:
                    pltpu.make_async_copy(
                        cut[n - 9], held_cut.at[slot], sems.at[slot]
                    ).start()

    for slot in range(4):
        here = slice(slot * 128, (slot + 1) * 128)

        @pl.when(info[slot] < 9)
        def _():
            pltpu.make_async_copy(rows[0], held.at[slot], sems.at[slot]).wait()
            for col in range(4):
                out[col // 2, here, col % 2 * 128 : (col % 2 + 1) * 128] = column_block(
                    held.at[slot], info[4 + slot * 4 + col]
                )

        @pl.when(info[slot] >= 9)
        def _():
            pltpu.make_async_copy(cut[0], held_cut.at[slot], sems.at[slot]).wait()
            for k in range(2):
                out[k, here, :] = held_cut[slot, :, k * 256 : (k + 1) * 256]


def pick(rows, cut, source, places):
    info = jnp.concatenate([source, places.reshape(-1)]).astype(jnp.int32)
    return pl.pallas_call(
        pick_kernel,
        out_shape=jax.ShapeDtypeStruct((2, 512, 256), jnp.float32),
        grid_spec=pltpu.PrefetchScalarGridSpec(
            num_scalar_prefetch=1,
            grid=(),
            in_specs=[pl.BlockSpec(memory_space=pl.ANY)] * 12,
            out_specs=pl.BlockSpec(memory_space=pltpu.VMEM),
            scratch_shapes=[
                pltpu.VMEM((4, 1024, 128), jnp.float32),
                pltpu.VMEM((4, 128, 512), jnp.float32),
                pltpu.SemaphoreType.DMA((4,)),
            ],
        ),
        compiler_params=pltpu.CompilerParams(vmem_limit_bytes=56 << 20),
        cost_estimate=pl.CostEstimate(flops=0, bytes_accessed=3 << 20, transcendentals=0),
        name="pick",
    )(info, *rows, *cut)


def two_halves(value):
    high = value.astype(jnp.bfloat16)
    return high, (value - high.astype(jnp.float32)).astype(jnp.bfloat16)


def halve_kernel(lower, near, lower_high, lower_low, near_high, near_low):
    lower_high[...], lower_low[...] = two_halves(lower[...])
    near_high[...], near_low[...] = two_halves(-near[...])


def halve(*values):
    whole = pl.BlockSpec(memory_space=pltpu.VMEM)
    return pl.pallas_call(
        halve_kernel,
        out_shape=[
            jax.ShapeDtypeStruct(value.shape, jnp.bfloat16) for value in values for _ in (0, 1)
        ],
        in_specs=[whole] * len(values),
        out_specs=[whole] * (2 * len(values)),
        compiler_params=pltpu.CompilerParams(vmem_limit_bytes=32 << 20),
        cost_estimate=pl.CostEstimate(flops=0, bytes_accessed=8 << 20, transcendentals=0),
        name="halve",
    )(*values)


def add_product(total, left, right):
    for one, two in ((left[0], right[0]), (left[0], right[1]), (left[1], right[0])):
        total += jnp.dot(one, two, preferred_element_type=jnp.float32)
    return total


def near_kernel(classes, *refs):
    restricted, high, low, panels = refs[0], refs[1], refs[2], refs[3:7]
    out, left, right_high, right_low, right, left_sems, sems, low_sems = refs[7:]

    def copies(n):
        piece = restricted.at[classes[n // 2 if n < 8 else n - 4], n % 2 if n < 8 else 0]
        yield pltpu.make_async_copy(piece, left.at[n], left_sems.at[n])
        if n < 8:
            rows = pl.ds(256 * n, 256)
            yield pltpu.make_async_copy(high.at[rows], right_high.at[n], sems.at[n])
            yield pltpu.make_async_copy(low.at[rows], right_low.at[n], low_sems.at[n])
        else:
            yield pltpu.make_async_copy(panels[n - 8], right.at[n - 8], sems.at[n])

    for n in range(12):
        for copy in copies(n):
            copy.start()
    for n in range(12):
        for copy in copies(n):
            copy.wait()
        panel = (right_high[n], right_low[n]) if n < 8 else two_halves(-right[n - 8])
        total = jnp.zeros(out.shape, jnp.float32) if n == 0 else out[...]
        out[...] = add_product(total, two_halves(left[n]), panel)


def near_product(restricted, halves, panels, classes):
    there = pl.BlockSpec(memory_space=pl.ANY)
    return pl.pallas_call(
        near_kernel,
        out_shape=jax.ShapeDtypeStruct((512, 256), jnp.float32),
        grid_spec=pltpu.PrefetchScalarGridSpec(
            num_scalar_prefetch=1,
            grid=(),
            in_specs=[there] * 7,
            out_specs=pl.BlockSpec(memory_space=pltpu.VMEM),
            scratch_shapes=[
                pltpu.VMEM((12, 512, 256), jnp.float32),
                pltpu.VMEM((8, 256, 256), jnp.bfloat16),
                pltpu.VMEM((8, 256, 256), jnp.bfloat16),
                pltpu.VMEM((4, 256, 256), jnp.float32),
                pltpu.SemaphoreType.DMA((12,)),
                pltpu.SemaphoreType.DMA((12,)),
                pltpu.SemaphoreType.DMA((8,)),
            ],
        ),
        compiler_params=pltpu.CompilerParams(vmem_limit_bytes=56 << 20),
        cost_estimate=pl.CostEstimate(
            flops=9 << 28, bytes_accessed=9 << 20, transcendentals=0
        ),
        name="near_product",
    )(classes, restricted, *halves, *panels)


def far_kernel(classes, *refs):
    restricted, panels, base, lower, out, share = (
        refs[0], refs[1:5], refs[5], refs[6:8], refs[8], refs[9:13]
    )
    left, right, held_high, held_low, left_sems, right_sems, sems = refs[13:]
    held = (held_high, held_low)

    def copies(n):
        piece = restricted.at[classes[4 + n], 1]
        yield pltpu.make_async_copy(piece, left.at[n], left_sems.at[n])
        yield pltpu.make_async_copy(panels[n], right.at[n], right_sems.at[n])

    for n in range(4):
        for copy in copies(n):
            copy.start()
    for k in range(2):
        pltpu.make_async_copy(lower[k], held[k], sems.at[k]).start()
    out[...] = base[...]
    for n in range(4):
        for copy in copies(n):
            copy.wait()
        out[...] = add_product(out[...], two_halves(left[n]), two_halves(-right[n]))
    for k in range(2):
        pltpu.make_async_copy(lower[k], held[k], sems.at[k]).wait()
    whole = two_halves(out[...])
    for j in range(4):
        share[j][...] = add_product(
            jnp.zeros((256, 256), jnp.float32), (held_high[j], held_low[j]), whole
        )


def far_product(restricted, panels, classes, base, lower):
    whole, there = pl.BlockSpec(memory_space=pltpu.VMEM), pl.BlockSpec(memory_space=pl.ANY)
    block = jax.ShapeDtypeStruct((256, 256), jnp.float32)
    return pl.pallas_call(
        far_kernel,
        out_shape=[jax.ShapeDtypeStruct((512, 256), jnp.float32)] + [block] * 4,
        grid_spec=pltpu.PrefetchScalarGridSpec(
            num_scalar_prefetch=1,
            grid=(),
            in_specs=[there] * 5 + [whole] + [there] * 2,
            out_specs=[whole] * 5,
            scratch_shapes=[
                pltpu.VMEM((4, 512, 256), jnp.float32),
                pltpu.VMEM((4, 256, 256), jnp.float32),
                pltpu.VMEM((4, 256, 512), jnp.bfloat16),
                pltpu.VMEM((4, 256, 512), jnp.bfloat16),
                pltpu.SemaphoreType.DMA((4,)),
                pltpu.SemaphoreType.DMA((4,)),
                pltpu.SemaphoreType.DMA((2,)),
            ],
        ),
        compiler_params=pltpu.CompilerParams(vmem_limit_bytes=56 << 20),
        cost_estimate=pl.CostEstimate(
            flops=3 << 29, bytes_accessed=6 << 20, transcendentals=0
        ),
        name="far_product",
    )(classes, restricted, *panels, base, *lower)


def on_device(parent_inverse, child_blocks, factor_rows, diag_inverse):
    child, half, x, y, core = (
        lax.axis_index(name) for name in ("zl", "zh", "x", "y", "core")
    )
    row_index, col_index = half * 4 + x, y * 2 + core
    lists = child_blocks.reshape(8, 4, 8)
    own_list = lax.dynamic_index_in_dim(lists, child, 0, keepdims=False)
    row_names = lax.dynamic_index_in_dim(own_list, row_index, 1, keepdims=False)
    col_names = lax.dynamic_index_in_dim(lists, col_index, 2, keepdims=False)
    row_alive = row_names >= 0
    col_place = jnp.where(col_names >= 0, col_names // 8, -1)
    offset = jnp.where(row_alive, row_names // 8 - child, 0)
    away = jnp.abs(offset)
    source = jnp.where(
        away > 4, away + 4, jnp.where(offset < 0, 2 * away - 1, 2 * away)
    )
    places = jnp.where(
        row_alive[:, None],
        lax.dynamic_index_in_dim(col_place, child, 0, keepdims=True),
        -1,
    )

    factor = factor_rows.reshape(512, 256)
    lower = lax.all_gather(factor, ("y", "core"), axis=0)
    near = lax.all_gather(factor, "x", axis=0).reshape(2048, 256)

    up = down = parent_inverse.reshape(1024, 128)
    rows = [up]
    for _ in range(4):
        up = lax.ppermute(up, "zl", [(i, i + 1) for i in range(7)])
        down = lax.ppermute(down, "zl", [(i + 1, i) for i in range(7)])
        up, down = lax.optimization_barrier((up, down))
        rows += [up, down]
    side = (child < 4).astype(jnp.int32)
    further = child + (1 - 2 * side) * jnp.arange(1, 4, dtype=jnp.int32)
    asked = jnp.take(col_place, jnp.clip(further, 0, 7), axis=0, mode="clip")
    cut = [
        lax.ppermute(
            part,
            "zl",
            [(i, i + d) for i in range(4, 8 - d)] + [(i, i - d) for i in range(d, 4)],
        )
        for d, part in zip((1, 2, 3), trim(up, down, side, asked))
    ]

    to_x = jnp.stack([(x + j) % 4 for j in range(4)])
    *cut, top, bottom, lower, near = lax.optimization_barrier(
        (*cut, factor[:256], factor[256:], lower, near)
    )

    restricted = pick(rows, cut, source, places)
    restricted, lower = lax.optimization_barrier((restricted, lower))
    far_lower = jnp.take(lower, (1 - half) * 4 + to_x, axis=0, mode="clip")
    far_lower, lower, near, top = lax.optimization_barrier(
        (far_lower.transpose(0, 2, 1), lower, near, top)
    )
    restricted = lax.all_gather(restricted, ("y", "core"), axis=0)
    own_lower = jnp.take(lower, half * 4 + to_x, axis=0, mode="clip")
    halves = halve(far_lower, near)
    top, bottom, own_lower, *halves = lax.optimization_barrier(
        (shift(top, "zh", 2, 1), bottom, own_lower, *halves)
    )
    bottom = shift(bottom, "zh", 2, 1)
    far_top = [top] + [shift(top, "x", 4, j) for j in (1, 2, 3)]

    number = jnp.arange(4, dtype=jnp.int32)
    classes = jnp.concatenate([half * 4 + number, (1 - half) * 4 + to_x]).astype(jnp.int32)
    inverse_local = near_product(restricted, halves[2:], far_top, classes)
    far_bottom = [bottom] + [shift(bottom, "x", 4, j) for j in (1, 2, 3)]
    inverse_local, *share = far_product(
        restricted, far_bottom, classes, inverse_local, halves[:2]
    )

    others = [shift(share[j], "x", 4, -j) for j in (1, 2, 3)]
    others[0], own_lower = lax.optimization_barrier((others[0], own_lower))
    other_half = share[0] + sum(others)
    share = [dot(own_lower[j], inverse_local, ((0,), (0,))) for j in range(4)]
    other_half, *share = lax.optimization_barrier((other_half, *share))
    other_half = shift(other_half, "zh", 2, 1)
    own_half = share[0] + sum(shift(share[j], "x", 4, -j) for j in (1, 2, 3))
    rest, own_half = lax.optimization_barrier((diag_inverse[0] - other_half, own_half))
    inverse_diag = (rest - own_half)[None]
    return inverse_local.reshape(1, 4, 1, 128, 256), inverse_diag


def solution(mesh):
    fine = Mesh(mesh.devices.reshape(8, 2, 4, 4, 2), ("zl", "zh", "x", "y", "core"))
    rows, cols = ("zh", "x"), ("y", "core")
    in_specs = (
        P("zl", rows, None, None, cols, None),
        P(),
        P("zl", None, rows, None, cols),
        P("zl", rows, cols),
    )
    out_specs = (P("zl", None, rows, None, cols), P("zl", rows, cols))
    return jax.shard_map(
        on_device, mesh=fine, in_specs=in_specs, out_specs=out_specs, check_vma=False
    )
```

```python
import functools

import jax
import jax.numpy as jnp
from jax import lax
from jax.experimental import pallas as pl
from jax.experimental.pallas import tpu as pltpu
from jax.sharding import Mesh, PartitionSpec as P

def shift(value, axis, count, step):
    return lax.ppermute(value, axis, [(i, (i - step) % count) for i in range(count)])


def dot(left, right, contract):
    return lax.dot_general(
        left,
        right,
        (contract, ((), ())),
        precision=lax.Precision.HIGH,
        preferred_element_type=jnp.float32,
    )


def column_block(row, place):
    found = row[pl.ds(jnp.maximum(place, 0), 128, stride=8), :]
    return jnp.where(place >= 0, found, 0.0)


def trim_kernel(info, up, down, *refs):
    outs, held, sem = refs[:3], refs[3], refs[4]
    for n, row in enumerate((up, down)):

        @pl.when(info[0] == n)
        def _():
            pltpu.make_async_copy(row, held, sem).start()

    pltpu.make_async_copy(up, held, sem).wait()
    for n, out in enumerate(outs):
        for col in range(4):
            out[:, col * 128 : (col + 1) * 128] = column_block(held, info[1 + n * 4 + col])


def trim(up, down, side, places):
    info = jnp.concatenate([side[None], places.reshape(-1)]).astype(jnp.int32)
    return pl.pallas_call(
        trim_kernel,
        out_shape=[jax.ShapeDtypeStruct((128, 512), jnp.float32)] * 3,
        grid_spec=pltpu.PrefetchScalarGridSpec(
            num_scalar_prefetch=1,
            grid=(),
            in_specs=[pl.BlockSpec(memory_space=pl.ANY)] * 2,
            out_specs=[pl.BlockSpec(memory_space=pltpu.VMEM)] * 3,
            scratch_shapes=[
                pltpu.VMEM((1024, 128), jnp.float32),
                pltpu.SemaphoreType.DMA,
            ],
        ),
        compiler_params=pltpu.CompilerParams(vmem_limit_bytes=16 << 20),
        cost_estimate=pl.CostEstimate(flops=0, bytes_accessed=5 << 18, transcendentals=0),
        name="trim",
    )(info, up, down)


def pick_kernel(info, *refs):
    rows, cut, out, held, held_cut, sems = refs[:9], refs[9:12], *refs[12:]
    for slot in range(4):
        for n in range(12):

            @pl.when(info[slot] == n)
            def _():
                if n < 9:
                    pltpu.make_async_copy(rows[n], held.at[slot], sems.at[slot]).start()
                else:
                    pltpu.make_async_copy(
                        cut[n - 9], held_cut.at[slot], sems.at[slot]
                    ).start()

    for slot in range(4):
        here = slice(slot * 128, (slot + 1) * 128)

        @pl.when(info[slot] < 9)
        def _():
            pltpu.make_async_copy(rows[0], held.at[slot], sems.at[slot]).wait()
            for col in range(4):
                out[col // 2, here, col % 2 * 128 : (col % 2 + 1) * 128] = column_block(
                    held.at[slot], info[4 + slot * 4 + col]
                )

        @pl.when(info[slot] >= 9)
        def _():
            pltpu.make_async_copy(cut[0], held_cut.at[slot], sems.at[slot]).wait()
            for k in range(2):
                out[k, here, :] = held_cut[slot, :, k * 256 : (k + 1) * 256]


def pick(rows, cut, source, places):
    info = jnp.concatenate([source, places.reshape(-1)]).astype(jnp.int32)
    return pl.pallas_call(
        pick_kernel,
        out_shape=jax.ShapeDtypeStruct((2, 512, 256), jnp.float32),
        grid_spec=pltpu.PrefetchScalarGridSpec(
            num_scalar_prefetch=1,
            grid=(),
            in_specs=[pl.BlockSpec(memory_space=pl.ANY)] * 12,
            out_specs=pl.BlockSpec(memory_space=pltpu.VMEM),
            scratch_shapes=[
                pltpu.VMEM((4, 1024, 128), jnp.float32),
                pltpu.VMEM((4, 128, 512), jnp.float32),
                pltpu.SemaphoreType.DMA((4,)),
            ],
        ),
        compiler_params=pltpu.CompilerParams(vmem_limit_bytes=56 << 20),
        cost_estimate=pl.CostEstimate(flops=0, bytes_accessed=3 << 20, transcendentals=0),
        name="pick",
    )(info, *rows, *cut)


def two_halves(value):
    high = value.astype(jnp.bfloat16)
    return high, (value - high.astype(jnp.float32)).astype(jnp.bfloat16)


def product_kernel(terms, count, last, classes, *refs):
    restricted, panels = refs[0], refs[1 : 1 + count]
    if last:
        base, lower, out, *share = refs[1 + count : 8 + count]
        left, right, left_sems, right_sems, held, sem = refs[8 + count :]
    else:
        out, left, right, left_sems, right_sems = refs[1 + count :]

    def copies(n):
        index, panel, start, k = terms[n]
        yield pltpu.make_async_copy(
            restricted.at[classes[index], k], left.at[n], left_sems.at[n]
        )
        yield pltpu.make_async_copy(
            panels[panel].at[pl.ds(start, 256)], right.at[n], right_sems.at[n]
        )

    for n in range(len(terms)):
        for copy in copies(n):
            copy.start()
    if last:
        held_copy = pltpu.make_async_copy(lower, held, sem)
        held_copy.start()
    for n in range(len(terms)):
        for copy in copies(n):
            copy.wait()
        if n > 0:
            total = out[...]
        elif last:
            total = base[...]
        else:
            total = jnp.zeros(out.shape, jnp.float32)
        lh, ll = two_halves(left[n])
        rh, rl = two_halves(right[n])
        for one, two in ((lh, rh), (lh, rl), (ll, rh)):
            total -= jnp.dot(one, two, preferred_element_type=jnp.float32)
        out[...] = total
    if last:
        held_copy.wait()
        rh, rl = two_halves(out[...])
        for j in range(4):
            lh, ll = two_halves(held[j])
            total = jnp.zeros((256, 256), jnp.float32)
            for one, two in ((lh, rh), (lh, rl), (ll, rh)):
                total += jnp.dot(one, two, preferred_element_type=jnp.float32)
            share[j][...] = total


def product(restricted, panels, classes, terms, base=None, lower=None):
    last = base is not None
    whole, there = pl.BlockSpec(memory_space=pltpu.VMEM), pl.BlockSpec(memory_space=pl.ANY)
    out_shape = [jax.ShapeDtypeStruct((512, 256), jnp.float32)]
    scratch = [
        pltpu.VMEM((len(terms), 512, 256), jnp.float32),
        pltpu.VMEM((len(terms), 256, 256), jnp.float32),
        pltpu.SemaphoreType.DMA((len(terms),)),
        pltpu.SemaphoreType.DMA((len(terms),)),
    ]
    if last:
        out_shape += [jax.ShapeDtypeStruct((256, 256), jnp.float32)] * 4
        scratch += [pltpu.VMEM((4, 256, 512), jnp.float32), pltpu.SemaphoreType.DMA]
    return pl.pallas_call(
        functools.partial(product_kernel, terms, len(panels), last),
        out_shape=out_shape,
        grid_spec=pltpu.PrefetchScalarGridSpec(
            num_scalar_prefetch=1,
            grid=(),
            in_specs=[there] * (1 + len(panels)) + [whole, there] * last,
            out_specs=[whole] * len(out_shape),
            scratch_shapes=scratch,
        ),
        compiler_params=pltpu.CompilerParams(vmem_limit_bytes=56 << 20),
        cost_estimate=pl.CostEstimate(
            flops=len(terms) * (3 << 26),
            bytes_accessed=len(terms) * (3 << 18),
            transcendentals=0,
        ),
        name="product",
    )(classes, restricted, *panels, *([base, lower] if last else []))


def on_device(parent_inverse, child_blocks, factor_rows, diag_inverse):
    child, half, x, y, core = (
        lax.axis_index(name) for name in ("zl", "zh", "x", "y", "core")
    )
    row_index, col_index = half * 4 + x, y * 2 + core
    lists = child_blocks.reshape(8, 4, 8)
    own_list = lax.dynamic_index_in_dim(lists, child, 0, keepdims=False)
    row_names = lax.dynamic_index_in_dim(own_list, row_index, 1, keepdims=False)
    col_names = lax.dynamic_index_in_dim(lists, col_index, 2, keepdims=False)
    row_alive = row_names >= 0
    col_place = jnp.where(col_names >= 0, col_names // 8, -1)
    offset = jnp.where(row_alive, row_names // 8 - child, 0)
    away = jnp.abs(offset)
    source = jnp.where(
        away > 4, away + 4, jnp.where(offset < 0, 2 * away - 1, 2 * away)
    )
    places = jnp.where(
        row_alive[:, None],
        lax.dynamic_index_in_dim(col_place, child, 0, keepdims=True),
        -1,
    )

    factor = factor_rows.reshape(512, 256)
    lower = lax.all_gather(factor, ("y", "core"), axis=0)
    near = lax.all_gather(factor, "x", axis=0).reshape(2048, 256)

    up = down = parent_inverse.reshape(1024, 128)
    rows = [up]
    for _ in range(4):
        up = lax.ppermute(up, "zl", [(i, i + 1) for i in range(7)])
        down = lax.ppermute(down, "zl", [(i + 1, i) for i in range(7)])
        up, down = lax.optimization_barrier((up, down))
        rows += [up, down]
    side = (child < 4).astype(jnp.int32)
    further = child + (1 - 2 * side) * jnp.arange(1, 4, dtype=jnp.int32)
    asked = jnp.take(col_place, jnp.clip(further, 0, 7), axis=0, mode="clip")
    cut = [
        lax.ppermute(
            part,
            "zl",
            [(i, i + d) for i in range(4, 8 - d)] + [(i, i - d) for i in range(d, 4)],
        )
        for d, part in zip((1, 2, 3), trim(up, down, side, asked))
    ]

    to_x = jnp.stack([(x + j) % 4 for j in range(4)])
    *cut, top, bottom, lower, near = lax.optimization_barrier(
        (*cut, factor[:256], factor[256:], lower, near)
    )

    restricted = pick(rows, cut, source, places)
    restricted, lower = lax.optimization_barrier((restricted, lower))
    far_lower = jnp.take(lower, (1 - half) * 4 + to_x, axis=0, mode="clip")
    far_lower, lower, top = lax.optimization_barrier((far_lower, lower, top))
    far_lower = far_lower.transpose(0, 2, 1)
    own_lower = jnp.take(lower, half * 4 + to_x, axis=0, mode="clip")
    restricted = lax.all_gather(restricted, ("y", "core"), axis=0)
    top, bottom, far_lower, own_lower = lax.optimization_barrier(
        (shift(top, "zh", 2, 1), bottom, far_lower, own_lower)
    )
    bottom = shift(bottom, "zh", 2, 1)
    far_top = [top] + [shift(top, "x", 4, j) for j in (1, 2, 3)]

    number = jnp.arange(4, dtype=jnp.int32)
    classes = jnp.concatenate([half * 4 + number, (1 - half) * 4 + to_x]).astype(jnp.int32)
    terms = [(j, 0, 512 * j + 256 * k, k) for j in range(4) for k in (0, 1)]
    terms += [(4 + j, 1 + j, 0, 0) for j in range(4)]
    (inverse_local,) = product(restricted, [near] + far_top, classes, terms)
    far_bottom = [bottom] + [shift(bottom, "x", 4, j) for j in (1, 2, 3)]
    terms = [(4 + j, j, 0, 1) for j in range(4)]
    inverse_local, *share = product(
        restricted, far_bottom, classes, terms, inverse_local, far_lower
    )

    others = [shift(share[j], "x", 4, -j) for j in (1, 2, 3)]
    others[0], own_lower = lax.optimization_barrier((others[0], own_lower))
    other_half = share[0] + sum(others)
    share = [dot(own_lower[j], inverse_local, ((0,), (0,))) for j in range(4)]
    other_half, *share = lax.optimization_barrier((other_half, *share))
    other_half = shift(other_half, "zh", 2, 1)
    own_half = share[0] + sum(shift(share[j], "x", 4, -j) for j in (1, 2, 3))
    rest, own_half = lax.optimization_barrier((diag_inverse[0] - other_half, own_half))
    inverse_diag = (rest - own_half)[None]
    return inverse_local.reshape(1, 4, 1, 128, 256), inverse_diag


def solution(mesh):
    fine = Mesh(mesh.devices.reshape(8, 2, 4, 4, 2), ("zl", "zh", "x", "y", "core"))
    rows, cols = ("zh", "x"), ("y", "core")
    in_specs = (
        P("zl", rows, None, None, cols, None),
        P(),
        P("zl", None, rows, None, cols),
        P("zl", rows, cols),
    )
    out_specs = (P("zl", None, rows, None, cols), P("zl", rows, cols))
    return jax.shard_map(
        on_device, mesh=fine, in_specs=in_specs, out_specs=out_specs, check_vma=False
    )
```

```python
import functools

import jax
import jax.numpy as jnp
from jax import lax
from jax.experimental import pallas as pl
from jax.experimental.pallas import tpu as pltpu
from jax.sharding import Mesh, PartitionSpec as P

def shift(value, axis, count, step):
    return lax.ppermute(value, axis, [(i, (i - step) % count) for i in range(count)])


def dot(left, right, contract):
    return lax.dot_general(
        left,
        right,
        (contract, ((), ())),
        precision=lax.Precision.HIGH,
        preferred_element_type=jnp.float32,
    )


def column_block(row, place):
    found = row[pl.ds(jnp.maximum(place, 0), 128, stride=8), :]
    return jnp.where(place >= 0, found, 0.0)


def trim_kernel(info, up, down, *refs):
    outs, held, sem = refs[:3], refs[3], refs[4]
    for n, row in enumerate((up, down)):

        @pl.when(info[0] == n)
        def _():
            pltpu.make_async_copy(row, held, sem).start()

    pltpu.make_async_copy(up, held, sem).wait()
    for n, out in enumerate(outs):
        for col in range(4):
            out[:, col * 128 : (col + 1) * 128] = column_block(held, info[1 + n * 4 + col])


def trim(up, down, side, places):
    info = jnp.concatenate([side[None], places.reshape(-1)]).astype(jnp.int32)
    return pl.pallas_call(
        trim_kernel,
        out_shape=[jax.ShapeDtypeStruct((128, 512), jnp.float32)] * 3,
        grid_spec=pltpu.PrefetchScalarGridSpec(
            num_scalar_prefetch=1,
            grid=(),
            in_specs=[pl.BlockSpec(memory_space=pl.ANY)] * 2,
            out_specs=[pl.BlockSpec(memory_space=pltpu.VMEM)] * 3,
            scratch_shapes=[
                pltpu.VMEM((1024, 128), jnp.float32),
                pltpu.SemaphoreType.DMA,
            ],
        ),
        compiler_params=pltpu.CompilerParams(vmem_limit_bytes=16 << 20),
        cost_estimate=pl.CostEstimate(flops=0, bytes_accessed=5 << 18, transcendentals=0),
        name="trim",
    )(info, up, down)


def pick_kernel(info, *refs):
    rows, cut, out, held, held_cut, sems = refs[:9], refs[9:12], *refs[12:]
    for slot in range(4):
        for n in range(12):

            @pl.when(info[slot] == n)
            def _():
                if n < 9:
                    pltpu.make_async_copy(rows[n], held.at[slot], sems.at[slot]).start()
                else:
                    pltpu.make_async_copy(
                        cut[n - 9], held_cut.at[slot], sems.at[slot]
                    ).start()

    for slot in range(4):
        here = slice(slot * 128, (slot + 1) * 128)

        @pl.when(info[slot] < 9)
        def _():
            pltpu.make_async_copy(rows[0], held.at[slot], sems.at[slot]).wait()
            for col in range(4):
                out[col // 2, here, col % 2 * 128 : (col % 2 + 1) * 128] = column_block(
                    held.at[slot], info[4 + slot * 4 + col]
                )

        @pl.when(info[slot] >= 9)
        def _():
            pltpu.make_async_copy(cut[0], held_cut.at[slot], sems.at[slot]).wait()
            for k in range(2):
                out[k, here, :] = held_cut[slot, :, k * 256 : (k + 1) * 256]


def pick(rows, cut, source, places):
    info = jnp.concatenate([source, places.reshape(-1)]).astype(jnp.int32)
    return pl.pallas_call(
        pick_kernel,
        out_shape=jax.ShapeDtypeStruct((2, 512, 256), jnp.float32),
        grid_spec=pltpu.PrefetchScalarGridSpec(
            num_scalar_prefetch=1,
            grid=(),
            in_specs=[pl.BlockSpec(memory_space=pl.ANY)] * 12,
            out_specs=pl.BlockSpec(memory_space=pltpu.VMEM),
            scratch_shapes=[
                pltpu.VMEM((4, 1024, 128), jnp.float32),
                pltpu.VMEM((4, 128, 512), jnp.float32),
                pltpu.SemaphoreType.DMA((4,)),
            ],
        ),
        compiler_params=pltpu.CompilerParams(vmem_limit_bytes=56 << 20),
        cost_estimate=pl.CostEstimate(flops=0, bytes_accessed=3 << 20, transcendentals=0),
        name="pick",
    )(info, *rows, *cut)


def two_halves(value):
    high = value.astype(jnp.bfloat16)
    return high, (value - high.astype(jnp.float32)).astype(jnp.bfloat16)


def product_kernel(terms, count, last, classes, *refs):
    restricted, panels = refs[0], refs[1 : 1 + count]
    if last:
        base, lower, out, *share = refs[1 + count : 8 + count]
        left, right, left_sems, right_sems, held, sem = refs[8 + count :]
    else:
        out, left, right, left_sems, right_sems = refs[1 + count :]

    def copies(n):
        index, panel, start, k = terms[n]
        yield pltpu.make_async_copy(
            restricted.at[classes[index], k], left.at[n], left_sems.at[n]
        )
        yield pltpu.make_async_copy(
            panels[panel].at[pl.ds(start, 256)], right.at[n], right_sems.at[n]
        )

    for n in range(len(terms)):
        for copy in copies(n):
            copy.start()
    if last:
        held_copy = pltpu.make_async_copy(lower, held, sem)
        held_copy.start()
    for n in range(len(terms)):
        for copy in copies(n):
            copy.wait()
        if n > 0:
            total = out[...]
        elif last:
            total = base[...]
        else:
            total = jnp.zeros(out.shape, jnp.float32)
        lh, ll = two_halves(left[n])
        rh, rl = two_halves(right[n])
        for one, two in ((lh, rh), (lh, rl), (ll, rh)):
            total -= jnp.dot(one, two, preferred_element_type=jnp.float32)
        out[...] = total
    if last:
        held_copy.wait()
        rh, rl = two_halves(out[...])
        for j in range(4):
            lh, ll = two_halves(held[j])
            total = jnp.zeros((256, 256), jnp.float32)
            for one, two in ((lh, rh), (lh, rl), (ll, rh)):
                total += jnp.dot(one, two, preferred_element_type=jnp.float32)
            share[j][...] = total


def product(restricted, panels, classes, terms, base=None, lower=None):
    last = base is not None
    whole, there = pl.BlockSpec(memory_space=pltpu.VMEM), pl.BlockSpec(memory_space=pl.ANY)
    out_shape = [jax.ShapeDtypeStruct((512, 256), jnp.float32)]
    scratch = [
        pltpu.VMEM((len(terms), 512, 256), jnp.float32),
        pltpu.VMEM((len(terms), 256, 256), jnp.float32),
        pltpu.SemaphoreType.DMA((len(terms),)),
        pltpu.SemaphoreType.DMA((len(terms),)),
    ]
    if last:
        out_shape += [jax.ShapeDtypeStruct((256, 256), jnp.float32)] * 4
        scratch += [pltpu.VMEM((4, 256, 512), jnp.float32), pltpu.SemaphoreType.DMA]
    return pl.pallas_call(
        functools.partial(product_kernel, terms, len(panels), last),
        out_shape=out_shape,
        grid_spec=pltpu.PrefetchScalarGridSpec(
            num_scalar_prefetch=1,
            grid=(),
            in_specs=[there] * (1 + len(panels)) + [whole, there] * last,
            out_specs=[whole] * len(out_shape),
            scratch_shapes=scratch,
        ),
        compiler_params=pltpu.CompilerParams(vmem_limit_bytes=56 << 20),
        cost_estimate=pl.CostEstimate(
            flops=len(terms) * (3 << 26),
            bytes_accessed=len(terms) * (3 << 18),
            transcendentals=0,
        ),
        name="product",
    )(classes, restricted, *panels, *([base, lower] if last else []))


def on_device(parent_inverse, child_blocks, factor_rows, diag_inverse):
    child, half, x, y, core = (
        lax.axis_index(name) for name in ("zl", "zh", "x", "y", "core")
    )
    row_index, col_index = half * 4 + x, y * 2 + core
    lists = child_blocks.reshape(8, 4, 8)
    own_list = lax.dynamic_index_in_dim(lists, child, 0, keepdims=False)
    row_names = lax.dynamic_index_in_dim(own_list, row_index, 1, keepdims=False)
    col_names = lax.dynamic_index_in_dim(lists, col_index, 2, keepdims=False)
    row_alive = row_names >= 0
    col_place = jnp.where(col_names >= 0, col_names // 8, -1)
    offset = jnp.where(row_alive, row_names // 8 - child, 0)
    away = jnp.abs(offset)
    source = jnp.where(
        away > 4, away + 4, jnp.where(offset < 0, 2 * away - 1, 2 * away)
    )
    places = jnp.where(
        row_alive[:, None],
        lax.dynamic_index_in_dim(col_place, child, 0, keepdims=True),
        -1,
    )

    factor = factor_rows.reshape(512, 256)
    lower = lax.all_gather(factor, ("y", "core"), axis=0)
    near = lax.all_gather(factor, "x", axis=0).reshape(2048, 256)

    up = down = parent_inverse.reshape(1024, 128)
    rows = [up]
    for _ in range(4):
        up = lax.ppermute(up, "zl", [(i, i + 1) for i in range(7)])
        down = lax.ppermute(down, "zl", [(i + 1, i) for i in range(7)])
        up, down = lax.optimization_barrier((up, down))
        rows += [up, down]
    side = (child < 4).astype(jnp.int32)
    further = child + (1 - 2 * side) * jnp.arange(1, 4, dtype=jnp.int32)
    asked = jnp.take(col_place, jnp.clip(further, 0, 7), axis=0, mode="clip")
    cut = [
        lax.ppermute(
            part,
            "zl",
            [(i, i + d) for i in range(4, 8 - d)] + [(i, i - d) for i in range(d, 4)],
        )
        for d, part in zip((1, 2, 3), trim(up, down, side, asked))
    ]

    to_x = jnp.stack([(x + j) % 4 for j in range(4)])
    *cut, top, bottom, lower, near = lax.optimization_barrier(
        (*cut, factor[:256], factor[256:], lower, near)
    )

    restricted = pick(rows, cut, source, places)
    restricted, lower = lax.optimization_barrier((restricted, lower))
    far_lower = jnp.take(lower, (1 - half) * 4 + to_x, axis=0, mode="clip")
    far_lower, lower, top = lax.optimization_barrier((far_lower, lower, top))
    far_lower = far_lower.transpose(0, 2, 1)
    own_lower = jnp.take(lower, half * 4 + to_x, axis=0, mode="clip")
    restricted = lax.all_gather(restricted, ("y", "core"), axis=0)
    number = jnp.arange(4, dtype=jnp.int32)
    classes = jnp.concatenate([half * 4 + number, (1 - half) * 4 + to_x]).astype(jnp.int32)
    top, bottom, far_lower, own_lower, classes = lax.optimization_barrier(
        (shift(top, "zh", 2, 1), bottom, far_lower, own_lower, classes)
    )
    bottom = shift(bottom, "zh", 2, 1)
    far_top = [top] + [shift(top, "x", 4, j) for j in (1, 2, 3)]

    terms = [(j, 0, 512 * j + 256 * k, k) for j in range(4) for k in (0, 1)]
    terms += [(4 + j, 1 + j, 0, 0) for j in range(4)]
    (inverse_local,) = product(restricted, [near] + far_top, classes, terms)
    far_bottom = [bottom] + [shift(bottom, "x", 4, j) for j in (1, 2, 3)]
    terms = [(4 + j, j, 0, 1) for j in range(4)]
    inverse_local, *share = product(
        restricted, far_bottom, classes, terms, inverse_local, far_lower
    )

    others = [shift(share[j], "x", 4, -j) for j in (1, 2, 3)]
    others[0], own_lower = lax.optimization_barrier((others[0], own_lower))
    other_half = share[0] + sum(others)
    share = [dot(own_lower[j], inverse_local, ((0,), (0,))) for j in range(4)]
    other_half, *share = lax.optimization_barrier((other_half, *share))
    other_half = shift(other_half, "zh", 2, 1)
    own_half = share[0] + sum(shift(share[j], "x", 4, -j) for j in (1, 2, 3))
    rest, own_half = lax.optimization_barrier((diag_inverse[0] - other_half, own_half))
    inverse_diag = (rest - own_half)[None]
    return inverse_local.reshape(1, 4, 1, 128, 256), inverse_diag


def solution(mesh):
    fine = Mesh(mesh.devices.reshape(8, 2, 4, 4, 2), ("zl", "zh", "x", "y", "core"))
    rows, cols = ("zh", "x"), ("y", "core")
    in_specs = (
        P("zl", rows, None, None, cols, None),
        P(),
        P("zl", None, rows, None, cols),
        P("zl", rows, cols),
    )
    out_specs = (P("zl", None, rows, None, cols), P("zl", rows, cols))
    return jax.shard_map(
        on_device, mesh=fine, in_specs=in_specs, out_specs=out_specs, check_vma=False
    )
```

```python
import functools

import jax
import jax.numpy as jnp
from jax import lax
from jax.experimental import pallas as pl
from jax.experimental.pallas import tpu as pltpu
from jax.sharding import Mesh, PartitionSpec as P

def shift(value, axis, count, step):
    return lax.ppermute(value, axis, [(i, (i - step) % count) for i in range(count)])


def dot(left, right, contract):
    return lax.dot_general(
        left,
        right,
        (contract, ((), ())),
        precision=lax.Precision.HIGH,
        preferred_element_type=jnp.float32,
    )


def column_block(row, place):
    found = row[pl.ds(jnp.maximum(place, 0), 128, stride=8), :]
    return jnp.where(place >= 0, found, 0.0)


def trim_kernel(info, up, down, *refs):
    outs, held, sem = refs[:3], refs[3], refs[4]
    for n, row in enumerate((up, down)):

        @pl.when(info[0] == n)
        def _():
            pltpu.make_async_copy(row, held, sem).start()

    pltpu.make_async_copy(up, held, sem).wait()
    for n, out in enumerate(outs):
        for col in range(4):
            out[:, col * 128 : (col + 1) * 128] = column_block(held, info[1 + n * 4 + col])


def trim(up, down, side, places):
    info = jnp.concatenate([side[None], places.reshape(-1)]).astype(jnp.int32)
    return pl.pallas_call(
        trim_kernel,
        out_shape=[jax.ShapeDtypeStruct((128, 512), jnp.float32)] * 3,
        grid_spec=pltpu.PrefetchScalarGridSpec(
            num_scalar_prefetch=1,
            grid=(),
            in_specs=[pl.BlockSpec(memory_space=pl.ANY)] * 2,
            out_specs=[pl.BlockSpec(memory_space=pltpu.VMEM)] * 3,
            scratch_shapes=[
                pltpu.VMEM((1024, 128), jnp.float32),
                pltpu.SemaphoreType.DMA,
            ],
        ),
        compiler_params=pltpu.CompilerParams(vmem_limit_bytes=16 << 20),
        cost_estimate=pl.CostEstimate(flops=0, bytes_accessed=5 << 18, transcendentals=0),
        name="trim",
    )(info, up, down)


def pick_kernel(info, *refs):
    rows, cut, out, held, held_cut, sems = refs[:9], refs[9:12], *refs[12:]
    for slot in range(4):
        for n in range(12):

            @pl.when(info[slot] == n)
            def _():
                if n < 9:
                    pltpu.make_async_copy(rows[n], held.at[slot], sems.at[slot]).start()
                else:
                    pltpu.make_async_copy(
                        cut[n - 9], held_cut.at[slot], sems.at[slot]
                    ).start()

    for slot in range(4):
        here = slice(slot * 128, (slot + 1) * 128)

        @pl.when(info[slot] < 9)
        def _():
            pltpu.make_async_copy(rows[0], held.at[slot], sems.at[slot]).wait()
            for col in range(4):
                out[col // 2, here, col % 2 * 128 : (col % 2 + 1) * 128] = column_block(
                    held.at[slot], info[4 + slot * 4 + col]
                )

        @pl.when(info[slot] >= 9)
        def _():
            pltpu.make_async_copy(cut[0], held_cut.at[slot], sems.at[slot]).wait()
            for k in range(2):
                out[k, here, :] = held_cut[slot, :, k * 256 : (k + 1) * 256]


def pick(rows, cut, source, places):
    info = jnp.concatenate([source, places.reshape(-1)]).astype(jnp.int32)
    return pl.pallas_call(
        pick_kernel,
        out_shape=jax.ShapeDtypeStruct((2, 512, 256), jnp.float32),
        grid_spec=pltpu.PrefetchScalarGridSpec(
            num_scalar_prefetch=1,
            grid=(),
            in_specs=[pl.BlockSpec(memory_space=pl.ANY)] * 12,
            out_specs=pl.BlockSpec(memory_space=pltpu.VMEM),
            scratch_shapes=[
                pltpu.VMEM((4, 1024, 128), jnp.float32),
                pltpu.VMEM((4, 128, 512), jnp.float32),
                pltpu.SemaphoreType.DMA((4,)),
            ],
        ),
        compiler_params=pltpu.CompilerParams(vmem_limit_bytes=56 << 20),
        cost_estimate=pl.CostEstimate(flops=0, bytes_accessed=3 << 20, transcendentals=0),
        name="pick",
    )(info, *rows, *cut)


def two_halves(value):
    high = value.astype(jnp.bfloat16)
    return high, (value - high.astype(jnp.float32)).astype(jnp.bfloat16)


def product_kernel(terms, count, last, classes, *refs):
    restricted, panels = refs[0], refs[1 : 1 + count]
    if last:
        base, lower, out, *share = refs[1 + count : 8 + count]
        left, right, left_sems, right_sems, held, sem = refs[8 + count :]
    else:
        out, left, right, left_sems, right_sems = refs[1 + count :]

    def copies(n):
        index, panel, start, k = terms[n]
        yield pltpu.make_async_copy(
            restricted.at[classes[index], k], left.at[n], left_sems.at[n]
        )
        yield pltpu.make_async_copy(
            panels[panel].at[pl.ds(start, 256)], right.at[n], right_sems.at[n]
        )

    for n in range(len(terms)):
        for copy in copies(n):
            copy.start()
    if last:
        held_copy = pltpu.make_async_copy(lower, held, sem)
        held_copy.start()
    for n in range(len(terms)):
        for copy in copies(n):
            copy.wait()
        if n > 0:
            total = out[...]
        elif last:
            total = base[...]
        else:
            total = jnp.zeros(out.shape, jnp.float32)
        lh, ll = two_halves(left[n])
        rh, rl = two_halves(right[n])
        for one, two in ((lh, rh), (lh, rl), (ll, rh)):
            total -= jnp.dot(one, two, preferred_element_type=jnp.float32)
        out[...] = total
    if last:
        held_copy.wait()
        rh, rl = two_halves(out[...])
        for j in range(4):
            lh, ll = two_halves(held[j])
            total = jnp.zeros((256, 256), jnp.float32)
            for one, two in ((lh, rh), (lh, rl), (ll, rh)):
                total += jnp.dot(one, two, preferred_element_type=jnp.float32)
            share[j][...] = total


def product(restricted, panels, classes, terms, base=None, lower=None):
    last = base is not None
    whole, there = pl.BlockSpec(memory_space=pltpu.VMEM), pl.BlockSpec(memory_space=pl.ANY)
    out_shape = [jax.ShapeDtypeStruct((512, 256), jnp.float32)]
    scratch = [
        pltpu.VMEM((len(terms), 512, 256), jnp.float32),
        pltpu.VMEM((len(terms), 256, 256), jnp.float32),
        pltpu.SemaphoreType.DMA((len(terms),)),
        pltpu.SemaphoreType.DMA((len(terms),)),
    ]
    if last:
        out_shape += [jax.ShapeDtypeStruct((256, 256), jnp.float32)] * 4
        scratch += [pltpu.VMEM((4, 256, 512), jnp.float32), pltpu.SemaphoreType.DMA]
    return pl.pallas_call(
        functools.partial(product_kernel, terms, len(panels), last),
        out_shape=out_shape,
        grid_spec=pltpu.PrefetchScalarGridSpec(
            num_scalar_prefetch=1,
            grid=(),
            in_specs=[there] * (1 + len(panels)) + [whole, there] * last,
            out_specs=[whole] * len(out_shape),
            scratch_shapes=scratch,
        ),
        compiler_params=pltpu.CompilerParams(vmem_limit_bytes=56 << 20),
        cost_estimate=pl.CostEstimate(
            flops=len(terms) * (3 << 26),
            bytes_accessed=len(terms) * (3 << 18),
            transcendentals=0,
        ),
        name="product",
    )(classes, restricted, *panels, *([base, lower] if last else []))


def on_device(parent_inverse, child_blocks, factor_rows, diag_inverse):
    child, half, x, y, core = (
        lax.axis_index(name) for name in ("zl", "zh", "x", "y", "core")
    )
    row_index, col_index = half * 4 + x, y * 2 + core
    lists = child_blocks.reshape(8, 4, 8)
    own_list = lax.dynamic_index_in_dim(lists, child, 0, keepdims=False)
    row_names = lax.dynamic_index_in_dim(own_list, row_index, 1, keepdims=False)
    col_names = lax.dynamic_index_in_dim(lists, col_index, 2, keepdims=False)
    row_alive = row_names >= 0
    col_place = jnp.where(col_names >= 0, col_names // 8, -1)
    offset = jnp.where(row_alive, row_names // 8 - child, 0)
    away = jnp.abs(offset)
    source = jnp.where(
        away > 4, away + 4, jnp.where(offset < 0, 2 * away - 1, 2 * away)
    )
    places = jnp.where(
        row_alive[:, None],
        lax.dynamic_index_in_dim(col_place, child, 0, keepdims=True),
        -1,
    )

    factor = factor_rows.reshape(512, 256)
    lower = lax.all_gather(factor, ("y", "core"), axis=0)
    near = lax.all_gather(factor, "x", axis=0).reshape(2048, 256)

    up = down = parent_inverse.reshape(1024, 128)
    rows = [up]
    for _ in range(4):
        up = lax.ppermute(up, "zl", [(i, i + 1) for i in range(7)])
        down = lax.ppermute(down, "zl", [(i + 1, i) for i in range(7)])
        up, down = lax.optimization_barrier((up, down))
        rows += [up, down]
    side = (child < 4).astype(jnp.int32)
    further = child + (1 - 2 * side) * jnp.arange(1, 4, dtype=jnp.int32)
    asked = jnp.take(col_place, jnp.clip(further, 0, 7), axis=0, mode="clip")
    cut = [
        lax.ppermute(
            part,
            "zl",
            [(i, i + d) for i in range(4, 8 - d)] + [(i, i - d) for i in range(d, 4)],
        )
        for d, part in zip((1, 2, 3), trim(up, down, side, asked))
    ]

    to_x = jnp.stack([(x + j) % 4 for j in range(4)])
    *cut, top, bottom, lower, near = lax.optimization_barrier(
        (*cut, factor[:256], factor[256:], lower, near)
    )

    restricted = pick(rows, cut, source, places)
    restricted, lower, top = lax.optimization_barrier((restricted, lower, top))
    far_lower = jnp.take(lower, (1 - half) * 4 + to_x, axis=0, mode="clip")
    far_lower = far_lower.transpose(0, 2, 1)
    own_lower = jnp.take(lower, half * 4 + to_x, axis=0, mode="clip")
    restricted = lax.all_gather(restricted, ("y", "core"), axis=0)
    number = jnp.arange(4, dtype=jnp.int32)
    classes = jnp.concatenate([half * 4 + number, (1 - half) * 4 + to_x]).astype(jnp.int32)
    top, bottom, far_lower, own_lower, classes = lax.optimization_barrier(
        (shift(top, "zh", 2, 1), bottom, far_lower, own_lower, classes)
    )
    bottom = shift(bottom, "zh", 2, 1)
    far_top = [top] + [shift(top, "x", 4, j) for j in (1, 2, 3)]

    terms = [(j, 0, 512 * j + 256 * k, k) for j in range(4) for k in (0, 1)]
    terms += [(4 + j, 1 + j, 0, 0) for j in range(4)]
    (inverse_local,) = product(restricted, [near] + far_top, classes, terms)
    far_bottom = [bottom] + [shift(bottom, "x", 4, j) for j in (1, 2, 3)]
    terms = [(4 + j, j, 0, 1) for j in range(4)]
    inverse_local, *share = product(
        restricted, far_bottom, classes, terms, inverse_local, far_lower
    )

    others = [shift(share[j], "x", 4, -j) for j in (1, 2, 3)]
    others[0], own_lower = lax.optimization_barrier((others[0], own_lower))
    other_half = share[0] + sum(others)
    share = [dot(own_lower[j], inverse_local, ((0,), (0,))) for j in range(4)]
    other_half, *share = lax.optimization_barrier((other_half, *share))
    other_half = shift(other_half, "zh", 2, 1)
    own_half = share[0] + sum(shift(share[j], "x", 4, -j) for j in (1, 2, 3))
    rest, own_half = lax.optimization_barrier((diag_inverse[0] - other_half, own_half))
    inverse_diag = (rest - own_half)[None]
    return inverse_local.reshape(1, 4, 1, 128, 256), inverse_diag


def solution(mesh):
    fine = Mesh(mesh.devices.reshape(8, 2, 4, 4, 2), ("zl", "zh", "x", "y", "core"))
    rows, cols = ("zh", "x"), ("y", "core")
    in_specs = (
        P("zl", rows, None, None, cols, None),
        P(),
        P("zl", None, rows, None, cols),
        P("zl", rows, cols),
    )
    out_specs = (P("zl", None, rows, None, cols), P("zl", rows, cols))
    return jax.shard_map(
        on_device, mesh=fine, in_specs=in_specs, out_specs=out_specs, check_vma=False
    )
```
